32 devices in a mesh: dp: 2 (over y), expert: 16 (over z, x, core).
Axes of the slice: x: 2, y: 2, z: 4, core: 2. Of those that a mesh axis runs over, the one named last changes fastest.
Arguments:
- latent: bfloat16 [4096, 4096], P(('dp', 'expert')), may hold values from -6 to 6
- dout: bfloat16 [4096, 4096], P(('dp', 'expert')), may hold values from -6 to 6
- routes: int32 [4096, 2], P(('dp', 'expert')), may hold values from 0 to 63, as said below
- gate_w: float32 [4096, 2], P(('dp', 'expert')), may hold values from 0.1 to 1
- norm_gain: float32 [4096], replicated, may hold values from 0.1 to 1.9
- w_gate_up: bfloat16 [16, 4096, 256], P('expert', 'dp'), may hold values from -0.09375 to 0.09375
- w_down: bfloat16 [16, 128, 4096], P('expert', None, 'dp'), may hold values from -0.1875 to 0.1875
Outputs:
- d_latent: bfloat16 [4096, 4096], P(('dp', 'expert'))
- grad_gate_up: bfloat16 [16, 4096, 256], P('expert', 'dp')
- grad_down: bfloat16 [16, 128, 4096], P('expert', None, 'dp')
The draws below stay inside these ranges and needn't reach their ends.
Inputs may be any that keep to these rules, and one draw needn't show every extreme that they name: `routes`: each patch names two different experts, at most one of them below 2. The patches of one device name no expert below 2 more than 4 times, and in every draw some expert below 2 is named exactly 4 times by the patches of every device of one index of dp.
All inputs are finite; a program needn't handle non-finite values.
Results may differ from the reference program's by a relative error of at most 0.013.
Values may be sent and summed in bfloat16 or wider, within the bound.
A program may use at most 64 MiB of HBM per device.

```python
import jax
import jax.numpy as jnp
from jax import lax

D = 4096
H = 1024
EXPERTS = 64
SLICES = 8
CAP = 4
P_DEV = 128
HID_DEV = 128
E_FL = 2
SLOTS = 16
TOKENS = 4096
N_DP = 2
N_EXPERT = 16


def draw_routes(key, part):
    blocks = N_DP * N_EXPERT
    keys = jax.random.split(key, 6)
    hot = jax.random.randint(keys[0], (N_DP,), 0, E_FL)
    hot_block = jnp.repeat(hot, N_EXPERT, total_repeat_length=blocks)
    counts = jax.random.randint(keys[1], (blocks, E_FL), 0, CAP // 2 + 1)
    counts = jnp.where(jnp.arange(E_FL)[None, :] == hot_block[:, None], CAP, counts)
    ends = jnp.cumsum(counts, axis=1)
    order = jax.vmap(lambda one: jax.random.permutation(one, P_DEV))(jax.random.split(keys[2], blocks))
    first = jnp.sum((order[:, :, None] >= ends[:, None, :]).astype(jnp.int32), axis=2)
    outside = jax.random.randint(keys[3], (blocks, P_DEV), E_FL, EXPERTS)
    first = jnp.where(first < E_FL, first, outside)
    raw = jax.random.randint(keys[4], (blocks, P_DEV), E_FL, EXPERTS - 1)
    second = jnp.where((first >= E_FL) & (raw >= first), raw + 1, raw)
    flip = jax.random.randint(keys[5], (blocks, P_DEV), 0, 2) == 1
    left = jnp.where(flip, second, first)
    right = jnp.where(flip, first, second)
    return jnp.stack([left, right], axis=2).reshape(blocks * P_DEV, 2).astype(jnp.int32)


def steps_of(rng, extent, shards, low, top_value):
    def one(dim, shards_of):
        steps = jax.random.uniform(jax.random.fold_in(jax.random.fold_in(rng, 6), dim), (shards_of,), jnp.float32, low / len(shards), top_value / len(shards))
        return jnp.repeat(jnp.exp(steps), extent[dim] // shards_of).reshape((-1,) + (1,) * (len(extent) - dim - 1))

    loudness = one(*shards[0])
    for cut in shards[1:]:
        loudness = loudness * one(*cut)
    return loudness


def scatter_about(rng, shape, scale, bound, pieces=(), kind=jnp.bfloat16):
    entries = scale * jax.random.normal(rng, shape, jnp.float32)
    if pieces:
        entries = entries * steps_of(rng, shape, pieces, -0.22, 0.18)
    return jnp.clip(entries, -bound, bound).astype(kind)


def setup_inputs(seed: int = 0) -> dict:
    splits = jax.random.split(jax.random.key(seed), 8)
    return {
        "latent": scatter_about(splits[0], (TOKENS, D), 1.0, 6.0, ((0, 32),)),
        "dout": scatter_about(splits[1], (TOKENS, D), 1.0, 6.0, ((0, 32),)),
        "routes": draw_routes(jax.random.fold_in(splits[7], 71), 0),
        "gate_w": jnp.clip(0.1 + 0.9 * jax.random.uniform(splits[3], (TOKENS, 2), jnp.float32) ** steps_of(splits[3], (TOKENS, 2), ((0, 32),), -0.2, 0.2), 0.1, 1.0),
        "norm_gain": jnp.clip(1.0 + 0.18 * jax.random.normal(splits[4], (D,), jnp.float32), 0.1, 1.9),
        "w_gate_up": scatter_about(splits[5], (SLOTS, D, 2 * HID_DEV), D ** -0.5, 0.09375, ((0, 16), (1, 2))),
        "w_down": scatter_about(splits[6], (SLOTS, HID_DEV, D), H ** -0.5, 0.1875, ((0, 16), (2, 2))),
    }


EPS = 1e-06

def expert_pass(rows_in, rows_dy, wgu, wd):
    hid = wd.shape[0]
    pre = jnp.dot(rows_in, wgu, preferred_element_type=jnp.float32)
    gate = pre[:, :hid]
    up = pre[:, hid:]
    sig = jax.nn.sigmoid(gate)
    act = gate * sig
    hidden = (act * up).astype(jnp.bfloat16)
    dh = jnp.dot(rows_dy, wd.T, preferred_element_type=jnp.float32)
    d_up = dh * act
    d_gate = dh * up * sig * (1.0 + gate * (1.0 - sig))
    d_pre = jnp.concatenate([d_gate, d_up], axis=1).astype(jnp.bfloat16)
    return (hidden, d_pre)

def group_work(xe, ye, wgu, wd):
    per = xe.shape[1]
    rows_in = xe.reshape(-1, D)
    rows_dy = ye.reshape(-1, D)
    hidden, d_pre = expert_pass(rows_in, rows_dy, wgu, wd)
    back = jnp.dot(d_pre, wgu.T, preferred_element_type=jnp.float32).astype(jnp.bfloat16)
    total_gu = jnp.zeros((D, 2 * HID_DEV), jnp.float32)
    total_d = jnp.zeros((HID_DEV, D), jnp.float32)
    for index in range(N_DP):
        low = index * per
        part_gu = jnp.dot(rows_in[low:low + per].T, d_pre[low:low + per], preferred_element_type=jnp.float32)
        part_d = jnp.dot(hidden[low:low + per].T, rows_dy[low:low + per], preferred_element_type=jnp.float32)
        part_gu = lax.optimization_barrier(part_gu.astype(jnp.bfloat16))
        part_d = lax.optimization_barrier(part_d.astype(jnp.bfloat16))
        total_gu = total_gu + part_gu.astype(jnp.float32)
        total_d = total_d + part_d.astype(jnp.float32)
    return (total_gu.astype(jnp.bfloat16), total_d.astype(jnp.bfloat16), back)

def reference(latent, dout, routes, gate_w, norm_gain, w_gate_up, w_down):
    values = latent.astype(jnp.float32)
    inverse = lax.rsqrt(lax.optimization_barrier(jnp.mean(values * values, axis=1, keepdims=True)) + EPS)
    scaled = values * inverse
    expert_in = (scaled * norm_gain[None, :]).astype(jnp.bfloat16)
    inside = routes < E_FL
    chosen = lax.optimization_barrier(jnp.sum(jnp.where(inside, routes, 0), axis=1)).astype(jnp.int32)
    present = jnp.any(inside, axis=1)
    weight = lax.optimization_barrier(jnp.sum(jnp.where(inside, gate_w, jnp.float32(0.0)), axis=1))
    grad_scale = (weight[:, None] * dout.astype(jnp.float32)).astype(jnp.bfloat16)
    blocks = N_DP * N_EXPERT
    onehot = ((chosen[:, None] == jnp.arange(E_FL, dtype=jnp.int32)[None, :]) & present[:, None]).astype(jnp.int32)
    ranks = jnp.cumsum(onehot.reshape(blocks, P_DEV, E_FL), axis=1) - 1
    slot = lax.optimization_barrier(jnp.sum(ranks * onehot.reshape(blocks, P_DEV, E_FL), axis=2)).reshape(-1).astype(jnp.int32)
    target = jnp.where(present, chosen * CAP + slot, E_FL * CAP).astype(jnp.int32)
    block_id = (jnp.arange(TOKENS, dtype=jnp.int32) // P_DEV).astype(jnp.int32)
    empty = jnp.zeros((blocks, E_FL * CAP + 1, D), jnp.bfloat16)
    buf_in = empty.at[block_id, target].set(expert_in)[:, :E_FL * CAP]
    buf_dy = empty.at[block_id, target].set(grad_scale)[:, :E_FL * CAP]

    def arrange(buf):
        shaped = buf.reshape(N_DP, N_EXPERT, E_FL, CAP, D).transpose(2, 0, 1, 3, 4)
        return shaped.reshape(E_FL, N_DP, N_EXPERT * CAP, D)
    arr_in = arrange(buf_in)
    arr_dy = arrange(buf_dy)
    grads_gu = []
    grads_d = []
    tables = []
    for expert in range(E_FL):
        xe = arr_in[expert]
        ye = arr_dy[expert]

        def run(weights):
            return group_work(xe, ye, weights[0], weights[1])
        lo = expert * SLICES
        out_gu, out_d, backs = lax.map(run, (w_gate_up[lo:lo + SLICES], w_down[lo:lo + SLICES]))
        grads_gu.append(out_gu)
        grads_d.append(out_d)
        summed = lax.optimization_barrier(jnp.sum(backs.astype(jnp.float32), axis=0)).astype(jnp.bfloat16)
        tables.append(summed.reshape(N_DP, N_EXPERT, CAP, D))
    table = jnp.stack(tables).transpose(1, 2, 0, 3, 4).reshape(blocks, E_FL * CAP, D)
    table = jnp.concatenate([table, jnp.zeros((blocks, 1, D), jnp.bfloat16)], axis=1)
    d_in = table[block_id, target]
    grad_in = d_in.astype(jnp.float32) * norm_gain[None, :]
    d_latent = inverse * (grad_in - scaled * lax.optimization_barrier(jnp.mean(grad_in * scaled, axis=1, keepdims=True)))
    return (d_latent.astype(jnp.bfloat16), jnp.concatenate(grads_gu, axis=0), jnp.concatenate(grads_d, axis=0))
```

```python
import functools

import jax
import jax.numpy as jnp
from jax import lax
from jax.experimental import pallas as pl
from jax.experimental.pallas import tpu as pltpu
from jax.sharding import PartitionSpec as P

SLICES = 8
CAP = 4
EPS = 1e-06
F32 = jnp.float32
BF = jnp.bfloat16


def kernel(n_dp, groups, lat, dout, routes, gate_w, gain, wgu, wd, out_lat, out_gu, out_d,
           inrow, dyrow, sendbuf, stage, gath, xs, ys, part, xr, bk, rb1, rb2, acc, mid, homest, homeb, fin, table,
           s1, r1, s2, r2, s3, r3, sx, rx, s4, r4, s5, r5, s6, r6):
    patches, width = lat.shape
    dw = width // n_dp
    half = dw // 2
    quarter = dw // 4
    slots = n_dp * groups
    nr = groups * CAP
    hid = wd.shape[1]
    d = lax.axis_index("dp")
    j = lax.axis_index("expert")
    hi = j // SLICES
    m = j % SLICES
    bit0 = m % 2
    bit1 = (m // 2) % 2
    bit2 = m // 4
    f0 = 1 - 2 * bit0
    f1 = 2 - 4 * bit1
    f2 = 4 - 8 * bit2
    planes = (m + f1, m + f2, m + f1 + f2)
    ms = d * groups + hi

    def dev(dd, jj):
        return {"dp": dd, "expert": jj}

    def slot_dev(t):
        p = (ms + t) % slots
        return p, dev(p // groups, (p % groups) * SLICES + m)

    def rcopy(src, dst, ss, rs, to):
        return pltpu.make_async_remote_copy(
            src_ref=src, dst_ref=dst, send_sem=ss, recv_sem=rs, device_id=to,
            device_id_type=pl.DeviceIdType.MESH)

    sib = dev(d, hi * SLICES + m + f0)
    plane_devs = [dev(d, hi * SLICES + q) for q in planes]
    barrier = pltpu.get_barrier_semaphore()
    for t in range(1, slots):
        pl.semaphore_signal(barrier, inc=1, device_id=slot_dev(t)[1], device_id_type=pl.DeviceIdType.MESH)
    for to in [sib] + plane_devs:
        pl.semaphore_signal(barrier, inc=1, device_id=to, device_id_type=pl.DeviceIdType.MESH)

    r = routes[...]
    g = gate_w[...]
    c0, c1 = r[:, 0:1], r[:, 1:2]
    in0, in1 = c0 < groups, c1 < groups
    chosen = jnp.where(in0, c0, jnp.where(in1, c1, -1)).astype(F32)
    weight = jnp.where(in0, g[:, 0:1], 0.0) + jnp.where(in1, g[:, 1:2], 0.0)
    lane = lax.broadcasted_iota(jnp.int32, (patches, 128), 1).astype(F32)
    onehot = jnp.where(chosen == lane, 1.0, 0.0)
    low = (lax.broadcasted_iota(jnp.int32, (patches, patches), 1)
           < lax.broadcasted_iota(jnp.int32, (patches, patches), 0))
    prefix = jnp.dot(jnp.where(low, 1.0, 0.0).astype(BF), onehot.astype(BF), preferred_element_type=F32)
    slot = jnp.sum(prefix * onehot, axis=1, keepdims=True)
    target = jnp.where(chosen >= 0.0, chosen * CAP + slot, -1.0)
    sel_t = jnp.where(target == lane, 1.0, 0.0)
    sel = sel_t.T
    w_rows = jnp.sum((sel_t * weight).T, axis=1, keepdims=True)[:nr]
    pick = sel[:nr].astype(BF)
    raw = jnp.dot(pick, lat[...], preferred_element_type=F32)
    inverse = lax.rsqrt(jnp.mean(raw * raw, axis=1, keepdims=True) + EPS)
    scaled = raw * inverse
    inrow[...] = scaled * gain[...]
    dyrow[...] = w_rows * jnp.dot(pick, dout[...], preferred_element_type=F32)
    for dd in range(n_dp):
        for e in range(groups):
            for k in range(4):
                src = inrow if k < 2 else dyrow
                lo = dd * dw + (k % 2) * half
                stage[CAP * k:CAP * (k + 1), :] = src[CAP * e:CAP * (e + 1), lo:lo + half]
            sendbuf[dd * groups + e] = stage[...].astype(BF)

    pl.semaphore_wait(barrier, slots + 3)
    first = []
    for t in range(1, slots):
        p, to = slot_dev(t)
        c = rcopy(sendbuf.at[p], gath.at[m, ms], s1.at[t], r1.at[t], to)
        c.start()
        first.append(c)
    gath[m, ms] = sendbuf[ms]
    for c in first:
        c.wait()
    sends = []
    for i in range(3):
        c = rcopy(gath.at[m], gath.at[m], s2.at[i], r2.at[i], plane_devs[i])
        c.start()
        sends.append(c)
    own = rcopy(gath.at[m], gath.at[m], s3.at[3], r3.at[3], sib)
    own.start()
    relay = [own]
    for i in range(3):
        sends[i].wait_recv()
        c = rcopy(gath.at[planes[i]], gath.at[planes[i]], s3.at[i], r3.at[i], sib)
        c.start()
        relay.append(c)
    for c in relay:
        c.wait_recv()

    row = lax.broadcasted_iota(jnp.int32, (64, 64), 0)
    col = lax.broadcasted_iota(jnp.int32, (64, 64), 1)
    perm = jnp.where(col == ((row // 4) % 4) * 16 + (row // 16) * 4 + row % 4, 1.0, 0.0).astype(BF)
    per = slots // 4

    def arrange(c, carry):
        block = gath[c // per, pl.ds((c % per) * 4, 4)].reshape(64, half)
        s = jnp.dot(perm, block, preferred_element_type=F32).astype(BF)
        at = pl.ds(pl.multiple_of(c * 16, 16), 16)
        xs[at, :half] = s[:16]
        xs[at, half:] = s[16:32]
        ys[at, :half] = s[32:48]
        ys[at, half:] = s[48:]
        return carry

    lax.fori_loop(0, SLICES * per, arrange, 0)
    part[:, :2 * hid] = jnp.dot(xs[...], wgu[0], preferred_element_type=F32)
    part[:, 2 * hid:] = lax.dot_general(ys[...], wd[0], (((1,), (1,)), ((), ())), preferred_element_type=F32)
    xch = []
    for t in range(1, n_dp):
        c = rcopy(part, xr.at[t - 1], sx.at[t - 1], rx.at[t - 1], dev((d + t) % n_dp, j))
        c.start()
        xch.append(c)
    for c in sends + relay:
        c.wait_send()
    total = part[...]
    for t in range(1, n_dp):
        xch[t - 1].wait_recv()
        total = total + xr[t - 1]
    gate, up, dh = total[:, :hid], total[:, hid:2 * hid], total[:, 2 * hid:]
    sig = jax.nn.sigmoid(gate)
    act = gate * sig
    hidden = (act * up).astype(BF)
    d_gate = dh * up * sig * (1.0 + gate * (1.0 - sig))
    d_pre = jnp.concatenate([d_gate, dh * act], axis=1).astype(BF)
    rows_m = slots * CAP
    bk[...] = lax.dot_general(d_pre, wgu[0], (((1,), (1,)), ((), ())),
                              preferred_element_type=F32).astype(BF).reshape(SLICES, rows_m, dw)
    mine = planes + (m,)
    to_sib = []
    for i in range(4):
        c = rcopy(bk.at[mine[i] + f0], rb1.at[i], s4.at[i], r4.at[i], sib)
        c.start()
        to_sib.append(c)
    over = lax.dot_general(xs[...], d_pre, (((0,), (0,)), ((), ())), preferred_element_type=F32)
    out_gu[0] = over.astype(BF)
    to_plane = []
    for i in range(4):
        to_sib[i].wait_recv()
        both = bk[mine[i]].astype(F32) + rb1[i].astype(F32)
        if i < 3:
            mid[i] = both.astype(BF)
            c = rcopy(mid.at[i], rb2.at[i], s5.at[i], r5.at[i], plane_devs[i])
            c.start()
            to_plane.append(c)
        else:
            acc[...] = both
    out_d[0] = lax.dot_general(hidden, ys[...], (((0,), (0,)), ((), ())), preferred_element_type=F32).astype(BF)
    for i in range(3):
        to_plane[i].wait_recv()
        acc[...] += rb2[i].astype(F32)
    for s in range(slots):
        for q in range(4):
            homest[CAP * q:CAP * (q + 1), :] = acc[CAP * s:CAP * (s + 1), q * quarter:(q + 1) * quarter]
        homeb[s] = homest[...].astype(BF)
    home = []
    for t in range(1, slots):
        p, to = slot_dev(t)
        c = rcopy(homeb.at[p], fin.at[ms], s6.at[t], r6.at[t], to)
        c.start()
        home.append(c)
    fin[ms] = homeb[ms]
    for c in xch + to_sib + to_plane:
        c.wait_send()
    for c in home:
        c.wait()
    for dd in range(n_dp):
        for e in range(groups):
            homest[...] = fin[dd * groups + e].astype(F32)
            for q in range(4):
                lo = dd * dw + q * quarter
                table[CAP * e:CAP * (e + 1), lo:lo + quarter] = homest[CAP * q:CAP * (q + 1), :]
    grad_in = table[...] * gain[...]
    d_rows = inverse * (grad_in - scaled * jnp.mean(grad_in * scaled, axis=1, keepdims=True))
    put = sel[:nr].astype(BF)
    out_lat[...] = lax.dot_general(put, d_rows.astype(BF), (((0,), (0,)), ((), ())),
                                   preferred_element_type=F32).astype(BF)


def body(latent, dout, routes, gate_w, norm_gain, w_gate_up, w_down):
    patches, width = latent.shape
    n_dp = lax.axis_size("dp")
    groups = lax.axis_size("expert") // SLICES
    slots = n_dp * groups
    nr = groups * CAP
    dw = width // n_dp
    hid = w_down.shape[1]
    rows = SLICES * slots * CAP
    rows_m = slots * CAP
    vm = pltpu.VMEM
    dma = pltpu.SemaphoreType.DMA
    pairs = []
    for n in (slots, 3, 4, max(n_dp - 1, 1), 4, 3, slots):
        pairs += [dma((n,)), dma((n,))]
    return pl.pallas_call(
        functools.partial(kernel, n_dp, groups),
        out_shape=(
            jax.ShapeDtypeStruct(latent.shape, BF),
            jax.ShapeDtypeStruct(w_gate_up.shape, BF),
            jax.ShapeDtypeStruct(w_down.shape, BF),
        ),
        in_specs=[pl.BlockSpec(memory_space=vm)] * 7,
        out_specs=(pl.BlockSpec(memory_space=vm),) * 3,
        scratch_shapes=[
            vm((nr, width), F32), vm((nr, width), F32),
            vm((slots, 16, dw // 2), BF), vm((16, dw // 2), F32),
            vm((SLICES, slots, 16, dw // 2), BF),
            vm((rows, dw), BF), vm((rows, dw), BF),
            vm((rows, 3 * hid), F32), vm((max(n_dp - 1, 1), rows, 3 * hid), F32),
            vm((SLICES, rows_m, dw), BF), vm((4, rows_m, dw), BF), vm((3, rows_m, dw), BF),
            vm((rows_m, dw), F32), vm((3, rows_m, dw), BF),
            vm((16, dw // 4), F32), vm((slots, 16, dw // 4), BF), vm((slots, 16, dw // 4), BF),
            vm((nr, width), F32),
        ] + pairs,
        compiler_params=pltpu.CompilerParams(
            collective_id=0, has_side_effects=True, vmem_limit_bytes=60 * 1024 * 1024),
    )(latent, dout, routes, gate_w, norm_gain.reshape(1, width), w_gate_up, w_down)


def solution(mesh):
    placed = (
        P(("dp", "expert"), None),
        P(("dp", "expert"), None),
        P(("dp", "expert"), None),
        P(("dp", "expert"), None),
        P(),
        P("expert", "dp", None),
        P("expert", None, "dp"),
    )
    return jax.shard_map(
        body,
        mesh=mesh,
        in_specs=placed,
        out_specs=(P(("dp", "expert"), None), P("expert", "dp", None), P("expert", None, "dp")),
        check_vma=False,
    )
```

```python
import functools

import jax
import jax.numpy as jnp
from jax import lax
from jax.experimental import pallas as pl
from jax.experimental.pallas import tpu as pltpu
from jax.sharding import PartitionSpec as P

SLICES = 8
CAP = 4
EPS = 1e-06
F32 = jnp.float32
BF = jnp.bfloat16


def kernel(n_dp, groups, lat_h, dout_h, routes, gate_w, gain, wgu_h, wd_h, out_rows, out_sel, out_gu, out_d,
           lat, dout, wgu, wd, ld, inrow, dyrow, sendbuf, stage, gath, xs, ys, part, xr, bk, rb1, rb2, acc, mid, homest, homeb, fin, table,
           s1, r1, s2, r2, s3, r3, sx, rx, s4, r4, s5, r5, s6, r6):
    patches, width = lat_h.shape
    dw = width // n_dp
    half = dw // 2
    quarter = dw // 4
    slots = n_dp * groups
    nr = groups * CAP
    hid = wd.shape[1]
    d = lax.axis_index("dp")
    j = lax.axis_index("expert")
    hi = j // SLICES
    m = j % SLICES
    bit0 = m % 2
    bit1 = (m // 2) % 2
    bit2 = m // 4
    f0 = 1 - 2 * bit0
    f1 = 2 - 4 * bit1
    f2 = 4 - 8 * bit2
    planes = (m + f1, m + f2, m + f1 + f2)
    ms = d * groups + hi

    def dev(dd, jj):
        return {"dp": dd, "expert": jj}

    def slot_dev(t):
        p = (ms + t) % slots
        return p, dev(p // groups, (p % groups) * SLICES + m)

    def rcopy(src, dst, ss, rs, to):
        return pltpu.make_async_remote_copy(
            src_ref=src, dst_ref=dst, send_sem=ss, recv_sem=rs, device_id=to,
            device_id_type=pl.DeviceIdType.MESH)

    sib = dev(d, hi * SLICES + m + f0)
    plane_devs = [dev(d, hi * SLICES + q) for q in planes]
    barrier = pltpu.get_barrier_semaphore()
    for t in range(1, slots):
        pl.semaphore_signal(barrier, inc=1, device_id=slot_dev(t)[1], device_id_type=pl.DeviceIdType.MESH)
    for to in [sib] + plane_devs:
        pl.semaphore_signal(barrier, inc=1, device_id=to, device_id_type=pl.DeviceIdType.MESH)

    loads = []
    for i, (a, b) in enumerate(((lat_h, lat), (dout_h, dout), (wgu_h, wgu), (wd_h, wd))):
        c = pltpu.make_async_copy(a, b, ld.at[i])
        c.start()
        loads.append(c)
    r = routes[...]
    g = gate_w[...]
    c0, c1 = r[0:1, :], r[1:2, :]
    in0, in1 = c0 < groups, c1 < groups
    chosen = jnp.where(in0, c0, jnp.where(in1, c1, -1)).astype(F32)
    weight = jnp.where(in0, g[0:1, :], 0.0) + jnp.where(in1, g[1:2, :], 0.0)
    place = lax.broadcasted_iota(jnp.int32, (128, patches), 0).astype(F32)
    onehot = jnp.where(chosen == place, 1.0, 0.0)
    before = (lax.broadcasted_iota(jnp.int32, (patches, patches), 0)
              < lax.broadcasted_iota(jnp.int32, (patches, patches), 1))
    prefix = jnp.dot(onehot.astype(BF), jnp.where(before, 1.0, 0.0).astype(BF), preferred_element_type=F32)
    slot = jnp.sum(prefix * onehot, axis=0, keepdims=True)
    target = jnp.where(chosen >= 0.0, chosen * CAP + slot, -1.0)
    sel = jnp.where(target == place, 1.0, 0.0)[:nr]
    out_sel[...] = sel
    w_rows = jnp.sum(sel * weight, axis=1, keepdims=True)
    pick = sel.astype(BF)
    loads[0].wait()
    loads[1].wait()
    raw = jnp.dot(pick, lat[...], preferred_element_type=F32)
    inverse = lax.rsqrt(jnp.mean(raw * raw, axis=1, keepdims=True) + EPS)
    scaled = raw * inverse
    inrow[...] = scaled * gain[...]
    dyrow[...] = w_rows * jnp.dot(pick, dout[...], preferred_element_type=F32)
    for dd in range(n_dp):
        for e in range(groups):
            for k in range(4):
                src = inrow if k < 2 else dyrow
                lo = dd * dw + (k % 2) * half
                stage[CAP * k:CAP * (k + 1), :] = src[CAP * e:CAP * (e + 1), lo:lo + half]
            sendbuf[dd * groups + e] = stage[...].astype(BF)

    pl.semaphore_wait(barrier, slots + 3)
    first = []
    for t in range(1, slots):
        p, to = slot_dev(t)
        c = rcopy(sendbuf.at[p], gath.at[m, ms], s1.at[t], r1.at[t], to)
        c.start()
        first.append(c)
    gath[m, ms] = sendbuf[ms]
    order = [t for t in range(slots) if t % groups == 0] + [t for t in range(slots) if t % groups]
    sends = []
    for t in order:
        at = (ms + slots - t) % slots
        if t:
            first[t - 1].wait_recv()
        for i in range(3):
            c = rcopy(gath.at[m, at], gath.at[m, at], s2.at[i * slots + t], r2.at[i * slots + t], plane_devs[i])
            c.start()
            sends.append((i, c))
    own = rcopy(gath.at[m], gath.at[m], s3.at[3], r3.at[3], sib)
    own.start()
    relay = [own]
    row = lax.broadcasted_iota(jnp.int32, (64, 64), 0)
    col = lax.broadcasted_iota(jnp.int32, (64, 64), 1)
    perm = jnp.where(col == ((row // 4) % 4) * 16 + (row // 16) * 4 + row % 4, 1.0, 0.0).astype(BF)
    per = slots // 4

    def arrange(c, carry):
        block = gath[c // per, pl.ds((c % per) * 4, 4)].reshape(64, half)
        s = jnp.dot(perm, block, preferred_element_type=F32).astype(BF)
        at = pl.ds(pl.multiple_of(c * 16, 16), 16)
        xs[at, :half] = s[:16]
        xs[at, half:] = s[16:32]
        ys[at, :half] = s[32:48]
        ys[at, half:] = s[48:]
        return carry

    pair_rows = 2 * slots * CAP
    xch = []
    for n in range(4):
        if n:
            for i, c in sends:
                if i == n - 1:
                    c.wait_recv()
            c = rcopy(gath.at[planes[n - 1]], gath.at[planes[n - 1]], s3.at[n - 1], r3.at[n - 1], sib)
            c.start()
            relay.append(c)
        relay[n].wait_recv()
        pair = (planes[n - 1] if n else m) // 2
        lax.fori_loop(pair * 2 * per, pair * 2 * per + 2 * per, arrange, 0)
        if n == 0:
            loads[2].wait()
            loads[3].wait()
        at = pl.ds(pl.multiple_of(pair * pair_rows, 16), pair_rows)
        part[pair, :, :2 * hid] = jnp.dot(xs[at, :], wgu[0], preferred_element_type=F32)
        part[pair, :, 2 * hid:] = lax.dot_general(ys[at, :], wd[0], (((1,), (1,)), ((), ())),
                                                  preferred_element_type=F32)
        for t in range(1, n_dp):
            k = (t - 1) * 4 + n
            c = rcopy(part.at[pair], xr.at[t - 1, pair], sx.at[k], rx.at[k], dev((d + t) % n_dp, j))
            c.start()
            xch.append(c)
    for c in first + [c for _, c in sends] + relay:
        c.wait_send()
    for c in xch:
        c.wait_recv()
    total = part[...].reshape(4 * pair_rows, 3 * hid)
    for t in range(1, n_dp):
        total = total + xr[t - 1].reshape(4 * pair_rows, 3 * hid)
    gate, up, dh = total[:, :hid], total[:, hid:2 * hid], total[:, 2 * hid:]
    sig = jax.nn.sigmoid(gate)
    act = gate * sig
    hidden = (act * up).astype(BF)
    d_gate = dh * up * sig * (1.0 + gate * (1.0 - sig))
    d_pre = jnp.concatenate([d_gate, dh * act], axis=1).astype(BF)
    rows_m = slots * CAP
    bk[...] = lax.dot_general(d_pre, wgu[0], (((1,), (1,)), ((), ())),
                              preferred_element_type=F32).astype(BF).reshape(SLICES, rows_m, dw)
    mine = planes + (m,)
    to_sib = []
    for i in range(4):
        c = rcopy(bk.at[mine[i] + f0], rb1.at[i], s4.at[i], r4.at[i], sib)
        c.start()
        to_sib.append(c)
    over = lax.dot_general(xs[...], d_pre, (((0,), (0,)), ((), ())), preferred_element_type=F32)
    out_gu[0] = over.astype(BF)
    to_plane = []
    for i in range(4):
        to_sib[i].wait_recv()
        both = bk[mine[i]].astype(F32) + rb1[i].astype(F32)
        if i < 3:
            mid[i] = both.astype(BF)
            c = rcopy(mid.at[i], rb2.at[i], s5.at[i], r5.at[i], plane_devs[i])
            c.start()
            to_plane.append(c)
        else:
            acc[...] = both
    out_d[0] = lax.dot_general(hidden, ys[...], (((0,), (0,)), ((), ())), preferred_element_type=F32).astype(BF)
    for i in range(3):
        to_plane[i].wait_recv()
        acc[...] += rb2[i].astype(F32)
    for s in range(slots):
        for q in range(4):
            homest[CAP * q:CAP * (q + 1), :] = acc[CAP * s:CAP * (s + 1), q * quarter:(q + 1) * quarter]
        homeb[s] = homest[...].astype(BF)
    home = []
    for t in range(1, slots):
        p, to = slot_dev(t)
        c = rcopy(homeb.at[p], fin.at[ms], s6.at[t], r6.at[t], to)
        c.start()
        home.append(c)
    fin[ms] = homeb[ms]
    for c in xch + to_sib + to_plane:
        c.wait_send()
    for c in home:
        c.wait()
    for dd in range(n_dp):
        for e in range(groups):
            homest[...] = fin[dd * groups + e].astype(F32)
            for q in range(4):
                lo = dd * dw + q * quarter
                table[CAP * e:CAP * (e + 1), lo:lo + quarter] = homest[CAP * q:CAP * (q + 1), :]
    grad_in = table[...] * gain[...]
    d_rows = inverse * (grad_in - scaled * jnp.mean(grad_in * scaled, axis=1, keepdims=True))
    out_rows[...] = d_rows


def finish(rows, sel, gu, dn, out_lat, out_gu, out_d, sem):
    a = pltpu.make_async_copy(gu, out_gu, sem.at[0])
    b = pltpu.make_async_copy(dn, out_d, sem.at[1])
    a.start()
    b.start()
    out_lat[...] = lax.dot_general(sel[...].astype(BF), rows[...].astype(BF), (((0,), (0,)), ((), ())),
                                   preferred_element_type=F32).astype(BF)
    a.wait()
    b.wait()


def body(latent, dout, routes, gate_w, norm_gain, w_gate_up, w_down):
    patches, width = latent.shape
    n_dp = lax.axis_size("dp")
    groups = lax.axis_size("expert") // SLICES
    slots = n_dp * groups
    nr = groups * CAP
    dw = width // n_dp
    hid = w_down.shape[1]
    rows = SLICES * slots * CAP
    rows_m = slots * CAP
    vm = pltpu.VMEM
    dma = pltpu.SemaphoreType.DMA
    pairs = []
    for n in (slots, 3 * slots, 4, 4 * max(n_dp - 1, 1), 4, 3, slots):
        pairs += [dma((n,)), dma((n,))]
    any_ = pl.BlockSpec(memory_space=pl.ANY)
    vms = pl.BlockSpec(memory_space=vm)
    d_rows, sel, gu, dn = pl.pallas_call(
        functools.partial(kernel, n_dp, groups),
        out_shape=(
            jax.ShapeDtypeStruct((nr, width), F32),
            jax.ShapeDtypeStruct((nr, patches), F32),
            jax.ShapeDtypeStruct(w_gate_up.shape, BF),
            jax.ShapeDtypeStruct(w_down.shape, BF),
        ),
        in_specs=[any_, any_, vms, vms, vms, any_, any_],
        out_specs=(vms,) * 4,
        scratch_shapes=[
            vm(latent.shape, BF), vm(dout.shape, BF), vm(w_gate_up.shape, BF), vm(w_down.shape, BF), dma((4,)),
            vm((nr, width), F32), vm((nr, width), F32),
            vm((slots, 16, dw // 2), BF), vm((16, dw // 2), F32),
            vm((SLICES, slots, 16, dw // 2), BF),
            vm((rows, dw), BF), vm((rows, dw), BF),
            vm((4, rows // 4, 3 * hid), F32), vm((max(n_dp - 1, 1), 4, rows // 4, 3 * hid), F32),
            vm((SLICES, rows_m, dw), BF), vm((4, rows_m, dw), BF), vm((3, rows_m, dw), BF),
            vm((rows_m, dw), F32), vm((3, rows_m, dw), BF),
            vm((16, dw // 4), F32), vm((slots, 16, dw // 4), BF), vm((slots, 16, dw // 4), BF),
            vm((nr, width), F32),
        ] + pairs,
        compiler_params=pltpu.CompilerParams(
            collective_id=0, has_side_effects=True, vmem_limit_bytes=60 * 1024 * 1024),
    )(latent, dout, routes.T, gate_w.T, norm_gain.reshape(1, width), w_gate_up, w_down)
    return pl.pallas_call(
        finish,
        out_shape=(
            jax.ShapeDtypeStruct(latent.shape, BF),
            jax.ShapeDtypeStruct(w_gate_up.shape, BF),
            jax.ShapeDtypeStruct(w_down.shape, BF),
        ),
        in_specs=[vms, vms, any_, any_],
        out_specs=(vms, any_, any_),
        scratch_shapes=[dma((2,))],
        compiler_params=pltpu.CompilerParams(vmem_limit_bytes=60 * 1024 * 1024),
    )(d_rows, sel, gu, dn)


def solution(mesh):
    placed = (
        P(("dp", "expert"), None),
        P(("dp", "expert"), None),
        P(("dp", "expert"), None),
        P(("dp", "expert"), None),
        P(),
        P("expert", "dp", None),
        P("expert", None, "dp"),
    )
    return jax.shard_map(
        body,
        mesh=mesh,
        in_specs=placed,
        out_specs=(P(("dp", "expert"), None), P("expert", "dp", None), P("expert", None, "dp")),
        check_vma=False,
    )
```

```python
import functools

import jax
import jax.numpy as jnp
from jax import lax
from jax.experimental import pallas as pl
from jax.experimental.pallas import tpu as pltpu
from jax.sharding import PartitionSpec as P

SLICES = 8
CAP = 4
EPS = 1e-06
F32 = jnp.float32
BF = jnp.bfloat16


def kernel(n_dp, groups, lat_h, dout_h, routes, gate_w, gain, wgu_h, wd_h, out_rows, out_sel, out_gu, out_d,
           lat, dout, wgu, wd, gus, dns, ld, inrow, dyrow, sendbuf, stage, gath, xs, ys, part, xr, bk, rb1, rb2, acc, mid, homest, homeb, fin, table,
           s1, r1, s2, r2, s3, r3, sx, rx, s4, r4, s5, r5, s6, r6):
    patches, width = lat_h.shape
    dw = width // n_dp
    half = dw // 2
    quarter = dw // 4
    slots = n_dp * groups
    nr = groups * CAP
    hid = wd.shape[1]
    d = lax.axis_index("dp")
    j = lax.axis_index("expert")
    hi = j // SLICES
    m = j % SLICES
    bit0 = m % 2
    bit1 = (m // 2) % 2
    bit2 = m // 4
    f0 = 1 - 2 * bit0
    f1 = 2 - 4 * bit1
    f2 = 4 - 8 * bit2
    planes = (m + f1, m + f2, m + f1 + f2)
    ms = d * groups + hi

    def dev(dd, jj):
        return {"dp": dd, "expert": jj}

    def slot_dev(t):
        p = (ms + t) % slots
        return p, dev(p // groups, (p % groups) * SLICES + m)

    def rcopy(src, dst, ss, rs, to):
        return pltpu.make_async_remote_copy(
            src_ref=src, dst_ref=dst, send_sem=ss, recv_sem=rs, device_id=to,
            device_id_type=pl.DeviceIdType.MESH)

    sib = dev(d, hi * SLICES + m + f0)
    plane_devs = [dev(d, hi * SLICES + q) for q in planes]
    barrier = pltpu.get_barrier_semaphore()
    for t in range(1, slots):
        pl.semaphore_signal(barrier, inc=1, device_id=slot_dev(t)[1], device_id_type=pl.DeviceIdType.MESH)
    for to in [sib] + plane_devs:
        pl.semaphore_signal(barrier, inc=1, device_id=to, device_id_type=pl.DeviceIdType.MESH)

    loads = []
    for i, (a, b) in enumerate(((lat_h, lat), (dout_h, dout), (wgu_h, wgu), (wd_h, wd))):
        c = pltpu.make_async_copy(a, b, ld.at[i])
        c.start()
        loads.append(c)
    r = routes[...]
    g = gate_w[...]
    c0, c1 = r[0:1, :], r[1:2, :]
    in0, in1 = c0 < groups, c1 < groups
    chosen = jnp.where(in0, c0, jnp.where(in1, c1, -1)).astype(F32)
    weight = jnp.where(in0, g[0:1, :], 0.0) + jnp.where(in1, g[1:2, :], 0.0)
    place = lax.broadcasted_iota(jnp.int32, (128, patches), 0).astype(F32)
    onehot = jnp.where(chosen == place, 1.0, 0.0)
    before = (lax.broadcasted_iota(jnp.int32, (patches, patches), 0)
              < lax.broadcasted_iota(jnp.int32, (patches, patches), 1))
    prefix = jnp.dot(onehot.astype(BF), jnp.where(before, 1.0, 0.0).astype(BF), preferred_element_type=F32)
    slot = jnp.sum(prefix * onehot, axis=0, keepdims=True)
    target = jnp.where(chosen >= 0.0, chosen * CAP + slot, -1.0)
    sel = jnp.where(target == place, 1.0, 0.0)[:nr]
    out_sel[...] = sel
    w_rows = jnp.sum(sel * weight, axis=1, keepdims=True)
    pick = sel.astype(BF)
    loads[0].wait()
    loads[1].wait()
    raw = jnp.dot(pick, lat[...], preferred_element_type=F32)
    inverse = lax.rsqrt(jnp.mean(raw * raw, axis=1, keepdims=True) + EPS)
    scaled = raw * inverse
    inrow[...] = scaled * gain[...]
    dyrow[...] = w_rows * jnp.dot(pick, dout[...], preferred_element_type=F32)
    for dd in range(n_dp):
        for e in range(groups):
            for k in range(4):
                src = inrow if k < 2 else dyrow
                lo = dd * dw + (k % 2) * half
                stage[CAP * k:CAP * (k + 1), :] = src[CAP * e:CAP * (e + 1), lo:lo + half]
            sendbuf[dd * groups + e] = stage[...].astype(BF)

    pl.semaphore_wait(barrier, slots + 3)
    first = []
    for t in range(1, slots):
        p, to = slot_dev(t)
        c = rcopy(sendbuf.at[p], gath.at[m, ms], s1.at[t], r1.at[t], to)
        c.start()
        first.append(c)
    gath[m, ms] = sendbuf[ms]
    order = [t for t in range(slots) if t % groups == 0] + [t for t in range(slots) if t % groups]
    sends = []
    for t in order:
        at = (ms + slots - t) % slots
        if t:
            first[t - 1].wait_recv()
        for i in range(3):
            c = rcopy(gath.at[m, at], gath.at[m, at], s2.at[i * slots + t], r2.at[i * slots + t], plane_devs[i])
            c.start()
            sends.append((i, c))
    own = rcopy(gath.at[m], gath.at[m], s3.at[3], r3.at[3], sib)
    own.start()
    relay = [own]
    row = lax.broadcasted_iota(jnp.int32, (64, 64), 0)
    col = lax.broadcasted_iota(jnp.int32, (64, 64), 1)
    perm = jnp.where(col == ((row // 4) % 4) * 16 + (row // 16) * 4 + row % 4, 1.0, 0.0).astype(BF)
    per = slots // 4

    def arrange(c, carry):
        block = gath[c // per, pl.ds((c % per) * 4, 4)].reshape(64, half)
        s = jnp.dot(perm, block, preferred_element_type=F32).astype(BF)
        at = pl.ds(pl.multiple_of(c * 16, 16), 16)
        xs[at, :half] = s[:16]
        xs[at, half:] = s[16:32]
        ys[at, :half] = s[32:48]
        ys[at, half:] = s[48:]
        return carry

    pair_rows = 2 * slots * CAP
    xch = []
    for n in range(4):
        if n:
            for i, c in sends:
                if i == n - 1:
                    c.wait_recv()
            c = rcopy(gath.at[planes[n - 1]], gath.at[planes[n - 1]], s3.at[n - 1], r3.at[n - 1], sib)
            c.start()
            relay.append(c)
        relay[n].wait_recv()
        pair = (planes[n - 1] if n else m) // 2
        lax.fori_loop(pair * 2 * per, pair * 2 * per + 2 * per, arrange, 0)
        if n == 0:
            loads[2].wait()
            loads[3].wait()
        at = pl.ds(pl.multiple_of(pair * pair_rows, 16), pair_rows)
        part[pair, :, :2 * hid] = jnp.dot(xs[at, :], wgu[0], preferred_element_type=F32)
        part[pair, :, 2 * hid:] = lax.dot_general(ys[at, :], wd[0], (((1,), (1,)), ((), ())),
                                                  preferred_element_type=F32)
        for t in range(1, n_dp):
            k = (t - 1) * 4 + n
            c = rcopy(part.at[pair], xr.at[t - 1, pair], sx.at[k], rx.at[k], dev((d + t) % n_dp, j))
            c.start()
            xch.append(c)
    for c in first + [c for _, c in sends] + relay:
        c.wait_send()
    for c in xch:
        c.wait_recv()
    total = part[...].reshape(4 * pair_rows, 3 * hid)
    for t in range(1, n_dp):
        total = total + xr[t - 1].reshape(4 * pair_rows, 3 * hid)
    gate, up, dh = total[:, :hid], total[:, hid:2 * hid], total[:, 2 * hid:]
    sig = jax.nn.sigmoid(gate)
    act = gate * sig
    hidden = (act * up).astype(BF)
    d_gate = dh * up * sig * (1.0 + gate * (1.0 - sig))
    d_pre = jnp.concatenate([d_gate, dh * act], axis=1).astype(BF)
    rows_m = slots * CAP
    bk[...] = lax.dot_general(d_pre, wgu[0], (((1,), (1,)), ((), ())),
                              preferred_element_type=F32).astype(BF).reshape(SLICES, rows_m, dw)
    mine = planes + (m,)
    to_sib = []
    for i in range(4):
        c = rcopy(bk.at[mine[i] + f0], rb1.at[i], s4.at[i], r4.at[i], sib)
        c.start()
        to_sib.append(c)
    dns[0] = lax.dot_general(hidden, ys[...], (((0,), (0,)), ((), ())), preferred_element_type=F32).astype(BF)
    w_d = pltpu.make_async_copy(dns, out_d, ld.at[4])
    w_d.start()
    to_plane = []
    for i in range(4):
        to_sib[i].wait_recv()
        both = bk[mine[i]].astype(F32) + rb1[i].astype(F32)
        if i < 3:
            mid[i] = both.astype(BF)
            c = rcopy(mid.at[i], rb2.at[i], s5.at[i], r5.at[i], plane_devs[i])
            c.start()
            to_plane.append(c)
        else:
            acc[...] = both
    over = lax.dot_general(xs[...], d_pre, (((0,), (0,)), ((), ())), preferred_element_type=F32)
    gus[0] = over.astype(BF)
    w_gu = pltpu.make_async_copy(gus, out_gu, ld.at[5])
    w_gu.start()
    for i in range(3):
        to_plane[i].wait_recv()
        acc[...] += rb2[i].astype(F32)
    for s in range(slots):
        for q in range(4):
            homest[CAP * q:CAP * (q + 1), :] = acc[CAP * s:CAP * (s + 1), q * quarter:(q + 1) * quarter]
        homeb[s] = homest[...].astype(BF)
    home = []
    for t in range(1, slots):
        p, to = slot_dev(t)
        c = rcopy(homeb.at[p], fin.at[ms], s6.at[t], r6.at[t], to)
        c.start()
        home.append(c)
    fin[ms] = homeb[ms]
    for c in xch + to_sib + to_plane:
        c.wait_send()
    for c in home:
        c.wait()
    for dd in range(n_dp):
        for e in range(groups):
            homest[...] = fin[dd * groups + e].astype(F32)
            for q in range(4):
                lo = dd * dw + q * quarter
                table[CAP * e:CAP * (e + 1), lo:lo + quarter] = homest[CAP * q:CAP * (q + 1), :]
    grad_in = table[...] * gain[...]
    d_rows = inverse * (grad_in - scaled * jnp.mean(grad_in * scaled, axis=1, keepdims=True))
    out_rows[...] = d_rows
    w_d.wait()
    w_gu.wait()


def finish(rows, sel, gu, dn, out_lat, out_gu, out_d, sem):
    a = pltpu.make_async_copy(gu, out_gu, sem.at[0])
    b = pltpu.make_async_copy(dn, out_d, sem.at[1])
    a.start()
    b.start()
    out_lat[...] = lax.dot_general(sel[...].astype(BF), rows[...].astype(BF), (((0,), (0,)), ((), ())),
                                   preferred_element_type=F32).astype(BF)
    a.wait()
    b.wait()


def body(latent, dout, routes, gate_w, norm_gain, w_gate_up, w_down):
    patches, width = latent.shape
    n_dp = lax.axis_size("dp")
    groups = lax.axis_size("expert") // SLICES
    slots = n_dp * groups
    nr = groups * CAP
    dw = width // n_dp
    hid = w_down.shape[1]
    rows = SLICES * slots * CAP
    rows_m = slots * CAP
    vm = pltpu.VMEM
    dma = pltpu.SemaphoreType.DMA
    pairs = []
    for n in (slots, 3 * slots, 4, 4 * max(n_dp - 1, 1), 4, 3, slots):
        pairs += [dma((n,)), dma((n,))]
    any_ = pl.BlockSpec(memory_space=pl.ANY)
    vms = pl.BlockSpec(memory_space=vm)
    d_rows, sel, gu, dn = pl.pallas_call(
        functools.partial(kernel, n_dp, groups),
        out_shape=(
            jax.ShapeDtypeStruct((nr, width), F32),
            jax.ShapeDtypeStruct((nr, patches), F32),
            jax.ShapeDtypeStruct(w_gate_up.shape, BF),
            jax.ShapeDtypeStruct(w_down.shape, BF),
        ),
        in_specs=[any_, any_, vms, vms, vms, any_, any_],
        out_specs=(vms, vms, any_, any_),
        scratch_shapes=[
            vm(latent.shape, BF), vm(dout.shape, BF), vm(w_gate_up.shape, BF), vm(w_down.shape, BF),
            vm(w_gate_up.shape, BF), vm(w_down.shape, BF), dma((6,)),
            vm((nr, width), F32), vm((nr, width), F32),
            vm((slots, 16, dw // 2), BF), vm((16, dw // 2), F32),
            vm((SLICES, slots, 16, dw // 2), BF),
            vm((rows, dw), BF), vm((rows, dw), BF),
            vm((4, rows // 4, 3 * hid), F32), vm((max(n_dp - 1, 1), 4, rows // 4, 3 * hid), F32),
            vm((SLICES, rows_m, dw), BF), vm((4, rows_m, dw), BF), vm((3, rows_m, dw), BF),
            vm((rows_m, dw), F32), vm((3, rows_m, dw), BF),
            vm((16, dw // 4), F32), vm((slots, 16, dw // 4), BF), vm((slots, 16, dw // 4), BF),
            vm((nr, width), F32),
        ] + pairs,
        compiler_params=pltpu.CompilerParams(
            collective_id=0, has_side_effects=True, vmem_limit_bytes=60 * 1024 * 1024),
    )(latent, dout, routes.T, gate_w.T, norm_gain.reshape(1, width), w_gate_up, w_down)
    return pl.pallas_call(
        finish,
        out_shape=(
            jax.ShapeDtypeStruct(latent.shape, BF),
            jax.ShapeDtypeStruct(w_gate_up.shape, BF),
            jax.ShapeDtypeStruct(w_down.shape, BF),
        ),
        in_specs=[vms] * 4,
        out_specs=(vms, any_, any_),
        scratch_shapes=[dma((2,))],
        compiler_params=pltpu.CompilerParams(vmem_limit_bytes=60 * 1024 * 1024),
    )(d_rows, sel, gu, dn)


def solution(mesh):
    placed = (
        P(("dp", "expert"), None),
        P(("dp", "expert"), None),
        P(("dp", "expert"), None),
        P(("dp", "expert"), None),
        P(),
        P("expert", "dp", None),
        P("expert", None, "dp"),
    )
    return jax.shard_map(
        body,
        mesh=mesh,
        in_specs=placed,
        out_specs=(P(("dp", "expert"), None), P("expert", "dp", None), P("expert", None, "dp")),
        check_vma=False,
    )
```

```python
import functools

import jax
import jax.numpy as jnp
from jax import lax
from jax.experimental import pallas as pl
from jax.experimental.pallas import tpu as pltpu
from jax.sharding import PartitionSpec as P

SLICES = 8
CAP = 4
EPS = 1e-06
F32 = jnp.float32
BF = jnp.bfloat16


def kernel(n_dp, groups, lat_h, dout_h, routes, gate_w, gain, wgu_h, wd_h, out_rows, out_sel, out_gu, out_d,
           lat, dout, wgu, wd, gus, dns, ld, inrow, dyrow, sendbuf, stage, gath, xs, ys, part, xr, bk, rb1, rb2, acc, mid, homest, homeb, fin, table,
           s1, r1, s2, r2, s3, r3, sx, rx, s4, r4, s5, r5, s6, r6):
    patches, width = lat_h.shape
    dw = width // n_dp
    half = dw // 2
    quarter = dw // 4
    slots = n_dp * groups
    nr = groups * CAP
    hid = wd.shape[1]
    d = lax.axis_index("dp")
    j = lax.axis_index("expert")
    hi = j // SLICES
    m = j % SLICES
    bit0 = m % 2
    bit1 = (m // 2) % 2
    bit2 = m // 4
    f0 = 1 - 2 * bit0
    f1 = 2 - 4 * bit1
    f2 = 4 - 8 * bit2
    planes = (m + f1, m + f2, m + f1 + f2)
    ms = d * groups + hi

    def dev(dd, jj):
        return {"dp": dd, "expert": jj}

    def slot_dev(t):
        p = (ms + t) % slots
        return p, dev(p // groups, (p % groups) * SLICES + m)

    def rcopy(src, dst, ss, rs, to):
        return pltpu.make_async_remote_copy(
            src_ref=src, dst_ref=dst, send_sem=ss, recv_sem=rs, device_id=to,
            device_id_type=pl.DeviceIdType.MESH)

    sib = dev(d, hi * SLICES + m + f0)
    plane_devs = [dev(d, hi * SLICES + q) for q in planes]
    barrier = pltpu.get_barrier_semaphore()
    for t in range(1, slots):
        pl.semaphore_signal(barrier, inc=1, device_id=slot_dev(t)[1], device_id_type=pl.DeviceIdType.MESH)
    for to in [sib] + plane_devs:
        pl.semaphore_signal(barrier, inc=1, device_id=to, device_id_type=pl.DeviceIdType.MESH)

    loads = []
    for i, (a, b) in enumerate(((lat_h, lat), (dout_h, dout), (wgu_h, wgu), (wd_h, wd))):
        c = pltpu.make_async_copy(a, b, ld.at[i])
        c.start()
        loads.append(c)
    r = routes[...]
    g = gate_w[...]
    c0, c1 = r[0:1, :], r[1:2, :]
    in0, in1 = c0 < groups, c1 < groups
    chosen = jnp.where(in0, c0, jnp.where(in1, c1, -1)).astype(F32)
    weight = jnp.where(in0, g[0:1, :], 0.0) + jnp.where(in1, g[1:2, :], 0.0)
    place = lax.broadcasted_iota(jnp.int32, (128, patches), 0).astype(F32)
    onehot = jnp.where(chosen == place, 1.0, 0.0)
    before = (lax.broadcasted_iota(jnp.int32, (patches, patches), 0)
              < lax.broadcasted_iota(jnp.int32, (patches, patches), 1))
    prefix = jnp.dot(onehot.astype(BF), jnp.where(before, 1.0, 0.0).astype(BF), preferred_element_type=F32)
    slot = jnp.sum(prefix * onehot, axis=0, keepdims=True)
    target = jnp.where(chosen >= 0.0, chosen * CAP + slot, -1.0)
    sel = jnp.where(target == place, 1.0, 0.0)[:nr]
    out_sel[...] = sel
    w_rows = jnp.sum(sel * weight, axis=1, keepdims=True)
    pick = sel.astype(BF)
    loads[0].wait()
    loads[1].wait()
    raw = jnp.dot(pick, lat[...], preferred_element_type=F32)
    inverse = lax.rsqrt(jnp.mean(raw * raw, axis=1, keepdims=True) + EPS)
    scaled = raw * inverse
    inrow[...] = scaled * gain[...]
    dyrow[...] = w_rows * jnp.dot(pick, dout[...], preferred_element_type=F32)
    for dd in range(n_dp):
        for e in range(groups):
            for k in range(4):
                src = inrow if k < 2 else dyrow
                lo = dd * dw + (k % 2) * half
                stage[CAP * k:CAP * (k + 1), :] = src[CAP * e:CAP * (e + 1), lo:lo + half]
            sendbuf[dd * groups + e] = stage[...].astype(BF)

    pl.semaphore_wait(barrier, slots + 3)
    first = []
    for t in range(1, slots):
        p, to = slot_dev(t)
        c = rcopy(sendbuf.at[p], gath.at[m, ms], s1.at[t], r1.at[t], to)
        c.start()
        first.append(c)
    gath[m, ms] = sendbuf[ms]
    order = [t for t in range(slots) if t % groups == 0] + [t for t in range(slots) if t % groups]
    sends = []
    for t in order:
        at = (ms + slots - t) % slots
        if t:
            first[t - 1].wait_recv()
        for i in range(3):
            c = rcopy(gath.at[m, at], gath.at[m, at], s2.at[i * slots + t], r2.at[i * slots + t], plane_devs[i])
            c.start()
            sends.append((i, c))
    own = rcopy(gath.at[m], gath.at[m], s3.at[3], r3.at[3], sib)
    own.start()
    relay = [own]
    row = lax.broadcasted_iota(jnp.int32, (64, 64), 0)
    col = lax.broadcasted_iota(jnp.int32, (64, 64), 1)
    perm = jnp.where(col == ((row // 4) % 4) * 16 + (row // 16) * 4 + row % 4, 1.0, 0.0).astype(BF)
    per = slots // 4

    def arrange(c, carry):
        block = gath[c // per, pl.ds((c % per) * 4, 4)].reshape(64, half)
        s = jnp.dot(perm, block, preferred_element_type=F32).astype(BF)
        at = pl.ds(pl.multiple_of(c * 16, 16), 16)
        xs[at, :half] = s[:16]
        xs[at, half:] = s[16:32]
        ys[at, :half] = s[32:48]
        ys[at, half:] = s[48:]
        return carry

    pair_rows = 2 * slots * CAP
    xch = []
    for n in range(4):
        if n:
            for i, c in sends:
                if i == n - 1:
                    c.wait_recv()
            c = rcopy(gath.at[planes[n - 1]], gath.at[planes[n - 1]], s3.at[n - 1], r3.at[n - 1], sib)
            c.start()
            relay.append(c)
        relay[n].wait_recv()
        pair = (planes[n - 1] if n else m) // 2
        lax.fori_loop(pair * 2 * per, pair * 2 * per + 2 * per, arrange, 0)
        if n == 0:
            loads[2].wait()
            loads[3].wait()
        at = pl.ds(pl.multiple_of(pair * pair_rows, 16), pair_rows)
        part[pair, :, :2 * hid] = jnp.dot(xs[at, :], wgu[0], preferred_element_type=F32)
        part[pair, :, 2 * hid:] = lax.dot_general(ys[at, :], wd[0], (((1,), (1,)), ((), ())),
                                                  preferred_element_type=F32)
        for t in range(1, n_dp):
            k = (t - 1) * 4 + n
            c = rcopy(part.at[pair], xr.at[t - 1, pair], sx.at[k], rx.at[k], dev((d + t) % n_dp, j))
            c.start()
            xch.append(c)
    for c in first + [c for _, c in sends] + relay:
        c.wait_send()
    for c in xch:
        c.wait_recv()
    total = part[...].reshape(4 * pair_rows, 3 * hid)
    for t in range(1, n_dp):
        total = total + xr[t - 1].reshape(4 * pair_rows, 3 * hid)
    gate, up, dh = total[:, :hid], total[:, hid:2 * hid], total[:, 2 * hid:]
    sig = jax.nn.sigmoid(gate)
    act = gate * sig
    hidden = (act * up).astype(BF)
    d_gate = dh * up * sig * (1.0 + gate * (1.0 - sig))
    d_pre = jnp.concatenate([d_gate, dh * act], axis=1).astype(BF)
    rows_m = slots * CAP
    mine = planes + (m,)
    to_sib = []
    for h in range(2):
        bk[h] = lax.dot_general(d_pre, wgu[0, h * half:(h + 1) * half, :], (((1,), (1,)), ((), ())),
                                preferred_element_type=F32).astype(BF).reshape(SLICES, rows_m, half)
        for i in range(4):
            k = h * 4 + i
            c = rcopy(bk.at[h, mine[i] + f0], rb1.at[h, i], s4.at[k], r4.at[k], sib)
            c.start()
            to_sib.append(c)
    to_plane = []
    for h in range(2):
        for i in range(4):
            to_sib[h * 4 + i].wait_recv()
            both = bk[h, mine[i]].astype(F32) + rb1[h, i].astype(F32)
            if i < 3:
                k = h * 3 + i
                mid[h, i] = both.astype(BF)
                c = rcopy(mid.at[h, i], rb2.at[h, i], s5.at[k], r5.at[k], plane_devs[i])
                c.start()
                to_plane.append(c)
            else:
                acc[:, h * half:(h + 1) * half] = both
    over = lax.dot_general(xs[...], d_pre, (((0,), (0,)), ((), ())), preferred_element_type=F32)
    gus[0] = over.astype(BF)
    w_gu = pltpu.make_async_copy(gus, out_gu, ld.at[5])
    w_gu.start()
    for h in range(2):
        for i in range(3):
            to_plane[h * 3 + i].wait_recv()
            acc[:, h * half:(h + 1) * half] += rb2[h, i].astype(F32)
    for s in range(slots):
        for q in range(4):
            homest[CAP * q:CAP * (q + 1), :] = acc[CAP * s:CAP * (s + 1), q * quarter:(q + 1) * quarter]
        homeb[s] = homest[...].astype(BF)
    home = []
    for t in range(1, slots):
        p, to = slot_dev(t)
        c = rcopy(homeb.at[p], fin.at[ms], s6.at[t], r6.at[t], to)
        c.start()
        home.append(c)
    fin[ms] = homeb[ms]
    dns[0] = lax.dot_general(hidden, ys[...], (((0,), (0,)), ((), ())), preferred_element_type=F32).astype(BF)
    w_d = pltpu.make_async_copy(dns, out_d, ld.at[4])
    w_d.start()
    for c in xch + to_sib + to_plane:
        c.wait_send()
    for c in home:
        c.wait()
    for dd in range(n_dp):
        for e in range(groups):
            homest[...] = fin[dd * groups + e].astype(F32)
            for q in range(4):
                lo = dd * dw + q * quarter
                table[CAP * e:CAP * (e + 1), lo:lo + quarter] = homest[CAP * q:CAP * (q + 1), :]
    grad_in = table[...] * gain[...]
    d_rows = inverse * (grad_in - scaled * jnp.mean(grad_in * scaled, axis=1, keepdims=True))
    out_rows[...] = d_rows
    w_d.wait()
    w_gu.wait()


def finish(rows, sel, gu, dn, out_lat, out_gu, out_d, gus, dns, lts, sem):
    cut = gu.shape[1] // 2
    wide = lts.shape[2]
    plan = []
    for k in range(2):
        at = pl.ds(k * cut, cut)
        plan.append((gu.at[:, at], gus.at[:, at], out_gu.at[:, at]))
    plan.append((dn, dns, out_d))
    loads = [pltpu.make_async_copy(a, b, sem.at[k]) for k, (a, b, _) in enumerate(plan)]
    stores = [pltpu.make_async_copy(b, c, sem.at[3 + k]) for k, (_, b, c) in enumerate(plan)]
    for c in loads:
        c.start()
    put = sel[...].astype(BF)
    for k in range(4):
        at = pl.ds(k * wide, wide)
        lts[k] = lax.dot_general(put, rows[:, at].astype(BF), (((0,), (0,)), ((), ())),
                                 preferred_element_type=F32).astype(BF)
        c = pltpu.make_async_copy(lts.at[k], out_lat.at[:, at], sem.at[6 + k])
        c.start()
        stores.append(c)
        if k < 3:
            loads[k].wait()
            stores[k].start()
    for c in stores:
        c.wait()


def body(latent, dout, routes, gate_w, norm_gain, w_gate_up, w_down):
    patches, width = latent.shape
    n_dp = lax.axis_size("dp")
    groups = lax.axis_size("expert") // SLICES
    slots = n_dp * groups
    nr = groups * CAP
    dw = width // n_dp
    hid = w_down.shape[1]
    rows = SLICES * slots * CAP
    rows_m = slots * CAP
    vm = pltpu.VMEM
    dma = pltpu.SemaphoreType.DMA
    pairs = []
    for n in (slots, 3 * slots, 4, 4 * max(n_dp - 1, 1), 8, 6, slots):
        pairs += [dma((n,)), dma((n,))]
    any_ = pl.BlockSpec(memory_space=pl.ANY)
    vms = pl.BlockSpec(memory_space=vm)
    d_rows, sel, gu, dn = pl.pallas_call(
        functools.partial(kernel, n_dp, groups),
        out_shape=(
            jax.ShapeDtypeStruct((nr, width), F32),
            jax.ShapeDtypeStruct((nr, patches), F32),
            jax.ShapeDtypeStruct(w_gate_up.shape, BF),
            jax.ShapeDtypeStruct(w_down.shape, BF),
        ),
        in_specs=[any_, any_, vms, vms, vms, any_, any_],
        out_specs=(vms, vms, any_, any_),
        scratch_shapes=[
            vm(latent.shape, BF), vm(dout.shape, BF), vm(w_gate_up.shape, BF), vm(w_down.shape, BF),
            vm(w_gate_up.shape, BF), vm(w_down.shape, BF), dma((6,)),
            vm((nr, width), F32), vm((nr, width), F32),
            vm((slots, 16, dw // 2), BF), vm((16, dw // 2), F32),
            vm((SLICES, slots, 16, dw // 2), BF),
            vm((rows, dw), BF), vm((rows, dw), BF),
            vm((4, rows // 4, 3 * hid), F32), vm((max(n_dp - 1, 1), 4, rows // 4, 3 * hid), F32),
            vm((2, SLICES, rows_m, dw // 2), BF), vm((2, 4, rows_m, dw // 2), BF), vm((2, 3, rows_m, dw // 2), BF),
            vm((rows_m, dw), F32), vm((2, 3, rows_m, dw // 2), BF),
            vm((16, dw // 4), F32), vm((slots, 16, dw // 4), BF), vm((slots, 16, dw // 4), BF),
            vm((nr, width), F32),
        ] + pairs,
        compiler_params=pltpu.CompilerParams(
            collective_id=0, has_side_effects=True, vmem_limit_bytes=60 * 1024 * 1024),
    )(latent, dout, routes.T, gate_w.T, norm_gain.reshape(1, width), w_gate_up, w_down)
    return pl.pallas_call(
        finish,
        out_shape=(
            jax.ShapeDtypeStruct(latent.shape, BF),
            jax.ShapeDtypeStruct(w_gate_up.shape, BF),
            jax.ShapeDtypeStruct(w_down.shape, BF),
        ),
        in_specs=[vms, vms, any_, any_],
        out_specs=(any_,) * 3,
        scratch_shapes=[vm(w_gate_up.shape, BF), vm(w_down.shape, BF), vm((4, patches, width // 4), BF), dma((10,))],
        compiler_params=pltpu.CompilerParams(vmem_limit_bytes=60 * 1024 * 1024),
    )(d_rows, sel, gu, dn)


def solution(mesh):
    placed = (
        P(("dp", "expert"), None),
        P(("dp", "expert"), None),
        P(("dp", "expert"), None),
        P(("dp", "expert"), None),
        P(),
        P("expert", "dp", None),
        P("expert", None, "dp"),
    )
    return jax.shard_map(
        body,
        mesh=mesh,
        in_specs=placed,
        out_specs=(P(("dp", "expert"), None), P("expert", "dp", None), P("expert", None, "dp")),
        check_vma=False,
    )
```

```python
import functools

import jax
import jax.numpy as jnp
from jax import lax
from jax.experimental import pallas as pl
from jax.experimental.pallas import tpu as pltpu
from jax.sharding import PartitionSpec as P

SLICES = 8
CAP = 4
EPS = 1e-06
F32 = jnp.float32
BF = jnp.bfloat16


def kernel(n_dp, groups, lat_h, dout_h, routes, gate_w, gain, wgu_h, wd_h, out_rows, out_sel, out_gu, out_d,
           lat, dout, wgu, wd, gus, dns, ld, inrow, dyrow, sendbuf, stage, gath, xs, ys, part, xr, bk, rb1, rb2, acc, mid, homest, homeb, fin, table,
           s1, r1, s2, r2, s3, r3, sx, rx, s4, r4, s5, r5, s6, r6):
    patches, width = lat_h.shape
    dw = width // n_dp
    half = dw // 2
    quarter = dw // 4
    slots = n_dp * groups
    nr = groups * CAP
    hid = wd.shape[1]
    d = lax.axis_index("dp")
    j = lax.axis_index("expert")
    hi = j // SLICES
    m = j % SLICES
    bit0 = m % 2
    bit1 = (m // 2) % 2
    bit2 = m // 4
    f0 = 1 - 2 * bit0
    f1 = 2 - 4 * bit1
    f2 = 4 - 8 * bit2
    planes = (m + f1, m + f2, m + f1 + f2)
    ms = d * groups + hi

    def dev(dd, jj):
        return {"dp": dd, "expert": jj}

    def slot_dev(t):
        p = (ms + t) % slots
        return p, dev(p // groups, (p % groups) * SLICES + m)

    def rcopy(src, dst, ss, rs, to):
        return pltpu.make_async_remote_copy(
            src_ref=src, dst_ref=dst, send_sem=ss, recv_sem=rs, device_id=to,
            device_id_type=pl.DeviceIdType.MESH)

    sib = dev(d, hi * SLICES + m + f0)
    plane_devs = [dev(d, hi * SLICES + q) for q in planes]
    barrier = pltpu.get_barrier_semaphore()
    for t in range(1, slots):
        pl.semaphore_signal(barrier, inc=1, device_id=slot_dev(t)[1], device_id_type=pl.DeviceIdType.MESH)
    for to in [sib] + plane_devs:
        pl.semaphore_signal(barrier, inc=1, device_id=to, device_id_type=pl.DeviceIdType.MESH)

    loads = []
    for i, (a, b) in enumerate(((lat_h, lat), (dout_h, dout), (wgu_h, wgu), (wd_h, wd))):
        c = pltpu.make_async_copy(a, b, ld.at[i])
        c.start()
        loads.append(c)
    r = routes[...]
    g = gate_w[...]
    c0, c1 = r[0:1, :], r[1:2, :]
    in0, in1 = c0 < groups, c1 < groups
    chosen = jnp.where(in0, c0, jnp.where(in1, c1, -1)).astype(F32)
    weight = jnp.where(in0, g[0:1, :], 0.0) + jnp.where(in1, g[1:2, :], 0.0)
    place = lax.broadcasted_iota(jnp.int32, (128, patches), 0).astype(F32)
    onehot = jnp.where(chosen == place, 1.0, 0.0)
    before = (lax.broadcasted_iota(jnp.int32, (patches, patches), 0)
              < lax.broadcasted_iota(jnp.int32, (patches, patches), 1))
    prefix = jnp.dot(onehot.astype(BF), jnp.where(before, 1.0, 0.0).astype(BF), preferred_element_type=F32)
    slot = jnp.sum(prefix * onehot, axis=0, keepdims=True)
    target = jnp.where(chosen >= 0.0, chosen * CAP + slot, -1.0)
    sel = jnp.where(target == place, 1.0, 0.0)[:nr]
    out_sel[...] = sel
    w_rows = jnp.sum(sel * weight, axis=1, keepdims=True)
    pick = sel.astype(BF)
    loads[0].wait()
    raw = jnp.dot(pick, lat[...], preferred_element_type=F32)
    inverse = lax.rsqrt(jnp.mean(raw * raw, axis=1, keepdims=True) + EPS)
    scaled = raw * inverse
    inrow[...] = scaled * gain[...]
    loads[1].wait()
    dyrow[...] = w_rows * jnp.dot(pick, dout[...], preferred_element_type=F32)
    for dd in range(n_dp):
        for e in range(groups):
            for k in range(4):
                src = inrow if k < 2 else dyrow
                lo = dd * dw + (k % 2) * half
                stage[CAP * k:CAP * (k + 1), :] = src[CAP * e:CAP * (e + 1), lo:lo + half]
            sendbuf[dd * groups + e] = stage[...].astype(BF)

    pl.semaphore_wait(barrier, slots + 3)
    first = []
    for t in range(1, slots):
        p, to = slot_dev(t)
        c = rcopy(sendbuf.at[p], gath.at[m, ms], s1.at[t], r1.at[t], to)
        c.start()
        first.append(c)
    gath[m, ms] = sendbuf[ms]
    order = [t for t in range(slots) if t % groups == 0] + [t for t in range(slots) if t % groups]
    sends = []
    for t in order:
        at = (ms + slots - t) % slots
        if t:
            first[t - 1].wait_recv()
        for i in (2, 0, 1):
            c = rcopy(gath.at[m, at], gath.at[m, at], s2.at[i * slots + t], r2.at[i * slots + t], plane_devs[i])
            c.start()
            sends.append((i, c))
    own = rcopy(gath.at[m], gath.at[m], s3.at[3], r3.at[3], sib)
    own.start()
    relay = [own]
    row = lax.broadcasted_iota(jnp.int32, (64, 64), 0)
    col = lax.broadcasted_iota(jnp.int32, (64, 64), 1)
    perm = jnp.where(col == ((row // 4) % 4) * 16 + (row // 16) * 4 + row % 4, 1.0, 0.0).astype(BF)
    per = slots // 4

    def arrange(c, carry):
        block = gath[c // per, pl.ds((c % per) * 4, 4)].reshape(64, half)
        s = jnp.dot(perm, block, preferred_element_type=F32).astype(BF)
        at = pl.ds(pl.multiple_of(c * 16, 16), 16)
        xs[at, :half] = s[:16]
        xs[at, half:] = s[16:32]
        ys[at, :half] = s[32:48]
        ys[at, half:] = s[48:]
        return carry

    pair_rows = 2 * slots * CAP
    xch = []
    for n in range(4):
        if n:
            for i, c in sends:
                if i == n - 1:
                    c.wait_recv()
            c = rcopy(gath.at[planes[n - 1]], gath.at[planes[n - 1]], s3.at[n - 1], r3.at[n - 1], sib)
            c.start()
            relay.append(c)
        relay[n].wait_recv()
        pair = (planes[n - 1] if n else m) // 2
        for k in range(2 * per):
            arrange(pair * 2 * per + k, 0)
        if n == 0:
            loads[2].wait()
            loads[3].wait()
        at = pl.ds(pl.multiple_of(pair * pair_rows, 16), pair_rows)
        part[pair, :, :2 * hid] = jnp.dot(xs[at, :], wgu[0], preferred_element_type=F32)
        part[pair, :, 2 * hid:] = lax.dot_general(ys[at, :], wd[0], (((1,), (1,)), ((), ())),
                                                  preferred_element_type=F32)
        for t in range(1, n_dp):
            k = (t - 1) * 4 + n
            c = rcopy(part.at[pair], xr.at[t - 1, pair], sx.at[k], rx.at[k], dev((d + t) % n_dp, j))
            c.start()
            xch.append(c)
    for c in first + [c for _, c in sends] + relay:
        c.wait_send()
    for c in xch:
        c.wait_recv()
    total = part[...].reshape(4 * pair_rows, 3 * hid)
    for t in range(1, n_dp):
        total = total + xr[t - 1].reshape(4 * pair_rows, 3 * hid)
    gate, up, dh = total[:, :hid], total[:, hid:2 * hid], total[:, 2 * hid:]
    sig = jax.nn.sigmoid(gate)
    act = gate * sig
    hidden = (act * up).astype(BF)
    d_gate = dh * up * sig * (1.0 + gate * (1.0 - sig))
    d_pre = jnp.concatenate([d_gate, dh * act], axis=1).astype(BF)
    rows_m = slots * CAP
    mine = planes + (m,)
    to_sib = []
    for h in range(2):
        bk[h] = lax.dot_general(d_pre, wgu[0, h * half:(h + 1) * half, :], (((1,), (1,)), ((), ())),
                                preferred_element_type=F32).astype(BF).reshape(SLICES, rows_m, half)
        for i in range(4):
            k = h * 4 + i
            c = rcopy(bk.at[h, mine[i] + f0], rb1.at[h, i], s4.at[k], r4.at[k], sib)
            c.start()
            to_sib.append(c)
    to_plane = []
    for h in range(2):
        for i in range(4):
            to_sib[h * 4 + i].wait_recv()
            both = bk[h, mine[i]].astype(F32) + rb1[h, i].astype(F32)
            if i < 3:
                k = h * 3 + i
                mid[h, i] = both.astype(BF)
                c = rcopy(mid.at[h, i], rb2.at[h, i], s5.at[k], r5.at[k], plane_devs[i])
                c.start()
                to_plane.append(c)
            else:
                acc[:, h * half:(h + 1) * half] = both
    over = lax.dot_general(xs[...], d_pre, (((0,), (0,)), ((), ())), preferred_element_type=F32)
    gus[0] = over.astype(BF)
    w_gu = pltpu.make_async_copy(gus, out_gu, ld.at[5])
    w_gu.start()
    for h in range(2):
        for i in range(3):
            to_plane[h * 3 + i].wait_recv()
            acc[:, h * half:(h + 1) * half] += rb2[h, i].astype(F32)
    for s in range(slots):
        for q in range(4):
            homest[CAP * q:CAP * (q + 1), :] = acc[CAP * s:CAP * (s + 1), q * quarter:(q + 1) * quarter]
        homeb[s] = homest[...].astype(BF)
    home = []
    for t in range(1, slots):
        p, to = slot_dev(t)
        c = rcopy(homeb.at[p], fin.at[ms], s6.at[t], r6.at[t], to)
        c.start()
        home.append(c)
    fin[ms] = homeb[ms]
    dns[0] = lax.dot_general(hidden, ys[...], (((0,), (0,)), ((), ())), preferred_element_type=F32).astype(BF)
    w_d = pltpu.make_async_copy(dns, out_d, ld.at[4])
    w_d.start()
    for c in xch + to_sib + to_plane:
        c.wait_send()
    for c in home:
        c.wait()
    for dd in range(n_dp):
        for e in range(groups):
            homest[...] = fin[dd * groups + e].astype(F32)
            for q in range(4):
                lo = dd * dw + q * quarter
                table[CAP * e:CAP * (e + 1), lo:lo + quarter] = homest[CAP * q:CAP * (q + 1), :]
    grad_in = table[...] * gain[...]
    d_rows = inverse * (grad_in - scaled * jnp.mean(grad_in * scaled, axis=1, keepdims=True))
    out_rows[...] = d_rows
    w_d.wait()
    w_gu.wait()


def finish(rows, sel, gu, dn, out_lat, out_gu, out_d, gus, dns, lts, sem):
    cut = gu.shape[1] // 2
    wide = lts.shape[2]
    plan = []
    for k in range(2):
        at = pl.ds(k * cut, cut)
        plan.append((gu.at[:, at], gus.at[:, at], out_gu.at[:, at]))
    plan.append((dn, dns, out_d))
    loads = [pltpu.make_async_copy(a, b, sem.at[k]) for k, (a, b, _) in enumerate(plan)]
    stores = [pltpu.make_async_copy(b, c, sem.at[3 + k]) for k, (_, b, c) in enumerate(plan)]
    for c in loads:
        c.start()
    put = sel[...].astype(BF)
    for k in range(4):
        at = pl.ds(k * wide, wide)
        lts[k] = lax.dot_general(put, rows[:, at].astype(BF), (((0,), (0,)), ((), ())),
                                 preferred_element_type=F32).astype(BF)
        c = pltpu.make_async_copy(lts.at[k], out_lat.at[:, at], sem.at[6 + k])
        c.start()
        stores.append(c)
        if k < 3:
            loads[k].wait()
            stores[k].start()
    for c in stores:
        c.wait()


def body(latent, dout, routes, gate_w, norm_gain, w_gate_up, w_down):
    patches, width = latent.shape
    n_dp = lax.axis_size("dp")
    groups = lax.axis_size("expert") // SLICES
    slots = n_dp * groups
    nr = groups * CAP
    dw = width // n_dp
    hid = w_down.shape[1]
    rows = SLICES * slots * CAP
    rows_m = slots * CAP
    vm = pltpu.VMEM
    dma = pltpu.SemaphoreType.DMA
    pairs = []
    for n in (slots, 3 * slots, 4, 4 * max(n_dp - 1, 1), 8, 6, slots):
        pairs += [dma((n,)), dma((n,))]
    any_ = pl.BlockSpec(memory_space=pl.ANY)
    vms = pl.BlockSpec(memory_space=vm)
    d_rows, sel, gu, dn = pl.pallas_call(
        functools.partial(kernel, n_dp, groups),
        out_shape=(
            jax.ShapeDtypeStruct((nr, width), F32),
            jax.ShapeDtypeStruct((nr, patches), F32),
            jax.ShapeDtypeStruct(w_gate_up.shape, BF),
            jax.ShapeDtypeStruct(w_down.shape, BF),
        ),
        in_specs=[any_, any_, vms, vms, vms, any_, any_],
        out_specs=(vms, vms, any_, any_),
        scratch_shapes=[
            vm(latent.shape, BF), vm(dout.shape, BF), vm(w_gate_up.shape, BF), vm(w_down.shape, BF),
            vm(w_gate_up.shape, BF), vm(w_down.shape, BF), dma((6,)),
            vm((nr, width), F32), vm((nr, width), F32),
            vm((slots, 16, dw // 2), BF), vm((16, dw // 2), F32),
            vm((SLICES, slots, 16, dw // 2), BF),
            vm((rows, dw), BF), vm((rows, dw), BF),
            vm((4, rows // 4, 3 * hid), F32), vm((max(n_dp - 1, 1), 4, rows // 4, 3 * hid), F32),
            vm((2, SLICES, rows_m, dw // 2), BF), vm((2, 4, rows_m, dw // 2), BF), vm((2, 3, rows_m, dw // 2), BF),
            vm((rows_m, dw), F32), vm((2, 3, rows_m, dw // 2), BF),
            vm((16, dw // 4), F32), vm((slots, 16, dw // 4), BF), vm((slots, 16, dw // 4), BF),
            vm((nr, width), F32),
        ] + pairs,
        compiler_params=pltpu.CompilerParams(
            collective_id=0, has_side_effects=True, vmem_limit_bytes=60 * 1024 * 1024),
    )(latent, dout, routes.T, gate_w.T, norm_gain.reshape(1, width), w_gate_up, w_down)
    return pl.pallas_call(
        finish,
        out_shape=(
            jax.ShapeDtypeStruct(latent.shape, BF),
            jax.ShapeDtypeStruct(w_gate_up.shape, BF),
            jax.ShapeDtypeStruct(w_down.shape, BF),
        ),
        in_specs=[vms, vms, any_, any_],
        out_specs=(any_,) * 3,
        scratch_shapes=[vm(w_gate_up.shape, BF), vm(w_down.shape, BF), vm((4, patches, width // 4), BF), dma((10,))],
        compiler_params=pltpu.CompilerParams(vmem_limit_bytes=60 * 1024 * 1024),
    )(d_rows, sel, gu, dn)


def solution(mesh):
    placed = (
        P(("dp", "expert"), None),
        P(("dp", "expert"), None),
        P(("dp", "expert"), None),
        P(("dp", "expert"), None),
        P(),
        P("expert", "dp", None),
        P("expert", None, "dp"),
    )
    return jax.shard_map(
        body,
        mesh=mesh,
        in_specs=placed,
        out_specs=(P(("dp", "expert"), None), P("expert", "dp", None), P("expert", None, "dp")),
        check_vma=False,
    )
```
